32 devices in a mesh: grp: 4 (over y, x), dev: 8 (over z, core).
Axes of the slice: x: 2, y: 2, z: 4, core: 2. Of those that a mesh axis runs over, the one named last changes fastest.
Arguments:
- pair_repr: bfloat16 [320, 320, 128], P(('grp', 'dev')), may hold values from -6 to 6
- w_left_gate: bfloat16 [128, 128], replicated, may hold values from -0.5 to 0.5
- w_left: bfloat16 [128, 128], replicated, may hold values from -0.5 to 0.5
- w_right_gate: bfloat16 [128, 128], replicated, may hold values from -0.5 to 0.5
- w_right: bfloat16 [128, 128], replicated, may hold values from -0.5 to 0.5
- w_out_gate: bfloat16 [128, 128], replicated, may hold values from -0.5 to 0.5
- w_out: bfloat16 [128, 128], replicated, may hold values from -0.5 to 0.5
- residue_mask: int32 [320], replicated, may hold values 0 or 1
Outputs:
- update: bfloat16 [320, 320, 128], P(('grp', 'dev'))
The draws below stay inside these ranges and needn't reach their ends.
Inputs may be any that keep to these rules, and one draw needn't show every extreme that they name: `residue_mask`: 1 marks a residue of the complex, 0 a padded token.
All inputs are finite; a program needn't handle non-finite values.
Results may differ from the reference program's by a relative error of at most 0.0087.
Values may be sent and summed in bfloat16 or wider, within the bound.
A program may use at most 128 MiB of HBM per device.

```python
import jax
import jax.numpy as jnp
from jax import lax

C = 128
CH = 128
TOKENS = 320
N_GRP = 4
N_DEV = 8


def set_ends(result, key, low, largest):
    longest = result.shape.index(max(result.shape))
    spots = []
    for shift in (0, 1):
        where = [jax.random.randint(jax.random.fold_in(key, axis), (), 0, length) for axis, length in enumerate(result.shape)]
        where[longest] = (where[longest] + shift) % result.shape[longest]
        spots.append(tuple(where))
    return result.at[spots[0]].set(low).at[spots[1]].set(largest)


def steps_of(stream_key, shape, pieces, low, top_value):
    level, own = 1.0, jax.random.fold_in(stream_key, 6)
    for dim, blocks in pieces:
        heights = jnp.exp(jax.random.uniform(jax.random.fold_in(own, dim), (blocks,), jnp.float32, low / len(pieces), top_value / len(pieces)))
        level = level * jnp.repeat(heights, shape[dim] // blocks).reshape([-1 if axis == dim else 1 for axis in range(len(shape))])
    return level


def noise(rng, shape, spread, bound, shards=(), held_as=jnp.bfloat16):
    values = jax.random.normal(rng, shape, jnp.float32) * spread
    if len(shards) > 0:
        values = steps_of(rng, shape, shards, -0.22, 0.18) * values
    return jnp.clip(values, min=-bound, max=bound).astype(held_as)


def setup_inputs(seed: int = 0) -> dict:
    streams_of = jax.random.split(jax.random.key(seed), 9)
    pair_repr = noise(streams_of[0], (TOKENS, TOKENS, C), 1.0, 6.0, ((0, 32),))
    w_left_gate = noise(streams_of[1], (C, CH), C ** -0.5, 0.5)
    w_left = noise(streams_of[2], (C, CH), C ** -0.5, 0.5)
    w_right_gate = noise(streams_of[3], (C, CH), C ** -0.5, 0.5)
    w_right = noise(streams_of[4], (C, CH), C ** -0.5, 0.5)
    w_out_gate = noise(streams_of[5], (C, C), C ** -0.5, 0.5)
    w_out = noise(streams_of[6], (CH, C), CH ** -0.5, 0.5)
    residue_mask = set_ends((jax.random.randint(streams_of[7], (TOKENS,), 0, 8) < 7).astype(jnp.int32), jax.random.fold_in(streams_of[7], 1), 0, 1)
    return dict(pair_repr=pair_repr, w_left_gate=w_left_gate, w_left=w_left, w_right_gate=w_right_gate, w_right=w_right, w_out_gate=w_out_gate, w_out=w_out, residue_mask=residue_mask)


EPSILON = 1e-05

def layer_norm(values, channel_axis):
    average = lax.optimization_barrier(jnp.mean(values, axis=channel_axis, keepdims=True))
    centered = values - average
    variance = lax.optimization_barrier(jnp.mean(centered * centered, axis=channel_axis, keepdims=True))
    return centered * lax.rsqrt(variance + EPSILON)

def gated_proj(normed, weight_gate, weight_value, pair_mask):
    normed_wide = normed.astype(jnp.float32)
    gate_logits = jnp.einsum('rkc,cf->frk', normed_wide, weight_gate.astype(jnp.float32))
    projected = jnp.einsum('rkc,cf->frk', normed_wide, weight_value.astype(jnp.float32))
    return (jax.nn.sigmoid(gate_logits) * projected * pair_mask[None]).astype(jnp.bfloat16)

def reference(pair_repr, w_left_gate, w_left, w_right_gate, w_right, w_out_gate, w_out, residue_mask):
    extent = pair_repr.shape[0]
    channels = pair_repr.shape[2]
    hidden = w_left.shape[1]
    blocks = N_GRP * N_DEV
    height = extent // blocks
    mask_float = residue_mask.astype(jnp.float32)
    stacked = pair_repr.reshape(blocks, height, extent, channels)
    row_masks = mask_float.reshape(blocks, height)

    def right_block(inputs):
        pair_rows, row_mask = inputs
        normed = layer_norm(pair_rows.astype(jnp.float32), 2).astype(jnp.bfloat16)
        pair_mask = row_mask[:, None] * mask_float[None, :]
        return gated_proj(normed, w_right_gate, w_right, pair_mask)
    right_rows = lax.map(right_block, (stacked, row_masks))
    right_all = jnp.transpose(right_rows, (1, 0, 2, 3)).reshape(hidden, extent, extent)

    def channel_product(operands):
        left_channel, right_channel = operands
        return jnp.dot(left_channel, right_channel.T, preferred_element_type=jnp.float32).astype(jnp.bfloat16)

    def finish(inputs):
        pair_rows, row_mask = inputs
        normed = layer_norm(pair_rows.astype(jnp.float32), 2).astype(jnp.bfloat16)
        pair_mask = row_mask[:, None] * mask_float[None, :]
        left_rows = gated_proj(normed, w_left_gate, w_left, pair_mask)
        out_gate = jax.nn.sigmoid(jnp.einsum('rkc,cd->rkd', normed.astype(jnp.float32), w_out_gate.astype(jnp.float32))).astype(jnp.bfloat16)
        product = lax.map(channel_product, (left_rows, right_all))
        normed_product = layer_norm(product.astype(jnp.float32), 0).astype(jnp.bfloat16)
        mixed_rows = jnp.einsum('crk,cd->rkd', normed_product.astype(jnp.float32), w_out.astype(jnp.float32))
        return (mixed_rows * out_gate.astype(jnp.float32)).astype(jnp.bfloat16)
    update = lax.map(finish, (stacked, row_masks))
    return update.reshape(extent, extent, channels)
```

```python
import functools

import jax
import jax.numpy as jnp
from jax import lax
from jax.experimental import pallas as pl
from jax.experimental.pallas import tpu as pltpu
from jax.sharding import PartitionSpec as P

EPSILON = 1e-05


def layer_norm(values, channel_axis):
    average = jnp.mean(values, axis=channel_axis, keepdims=True)
    centered = values - average
    variance = jnp.mean(centered * centered, axis=channel_axis, keepdims=True)
    return centered * lax.rsqrt(variance + EPSILON)


def gated_proj(normed, weight_gate, weight_value, pair_mask):
    gate_logits = jnp.einsum("rkc,cf->frk", normed, weight_gate, preferred_element_type=jnp.float32)
    projected = jnp.einsum("rkc,cf->frk", normed, weight_value, preferred_element_type=jnp.float32)
    return (jax.nn.sigmoid(gate_logits) * projected * pair_mask[None]).astype(jnp.bfloat16)


def local(pair_repr, w_left_gate, w_left, w_right_gate, w_right, w_out_gate, w_out, residue_mask):
    height = pair_repr.shape[0]
    row_start = (lax.axis_index("grp") * lax.axis_size("dev") + lax.axis_index("dev")) * height
    mask_float = residue_mask.astype(jnp.float32)
    row_mask = lax.dynamic_slice_in_dim(mask_float, row_start, height)
    pair_mask = row_mask[:, None] * mask_float[None, :]
    normed = layer_norm(pair_repr.astype(jnp.float32), 2).astype(jnp.bfloat16)
    left_rows = gated_proj(normed, w_left_gate, w_left, pair_mask)
    right_rows = gated_proj(normed, w_right_gate, w_right, pair_mask)
    out_gate = jax.nn.sigmoid(
        jnp.einsum("rkc,cd->rkd", normed, w_out_gate, preferred_element_type=jnp.float32)
    ).astype(jnp.bfloat16)
    left_cols, right_cols = (
        lax.all_to_all(left_rows, ("grp", "dev"), split_axis=0, concat_axis=1, tiled=True),
        lax.all_to_all(right_rows, ("grp", "dev"), split_axis=0, concat_axis=1, tiled=True),
    )
    product = jnp.einsum(
        "crk,csk->crs", left_cols, right_cols, preferred_element_type=jnp.float32
    ).astype(jnp.bfloat16)
    finish_product = lax.all_to_all(
        product, ("grp", "dev"), split_axis=1, concat_axis=0, tiled=True
    )
    normed_product = layer_norm(finish_product.astype(jnp.float32), 0).astype(jnp.bfloat16)
    mixed_rows = jnp.einsum(
        "crk,cd->rkd", normed_product, w_out, preferred_element_type=jnp.float32
    )
    return (mixed_rows * out_gate).astype(jnp.bfloat16)


MESH = pl.DeviceIdType.MESH


def sigmoid(x):
    return 1.0 / (1.0 + jnp.exp(-x))


def fused_kernel(
    n_grp, n_dev,
    x_ref, wlg_ref, wl_ref, wrg_ref, wr_ref, wog_ref, wo_ref, mask_ref, mask_s,
    out_ref,
    nbuf, r_src, l_src, p_src, r_buf, l_buf, p_buf, stage, l_mat, r_mat, y_buf,
    ra_send, l_send, p_send, z_send, r_recv, l_recv, p_recv, loc_sem,
):
    rows, tokens, chans = x_ref.shape
    half = rows // 2
    n_plane, _, ch, width = r_src.shape
    nz = n_dev // 2
    main = tokens // 128 * 128
    tail = tokens - main
    tiles = main // 128
    plane_rows = n_plane * rows
    grp = lax.axis_index("grp")
    dev = lax.axis_index("dev")
    z = dev // 2
    core = lax.rem(dev, 2)
    q = grp * 2 + core

    def plane_peer(other):
        return (other // 2, z * 2 + lax.rem(other, 2))

    def other_of(o):
        return lax.rem(q + o, n_plane)

    barrier = pltpu.get_barrier_semaphore()

    @pl.loop(1, n_plane)
    def _(o):
        pl.semaphore_signal(barrier, inc=1, device_id=plane_peer(other_of(o)), device_id_type=MESH)

    @pl.when(z > 0)
    def _():
        pl.semaphore_signal(barrier, inc=1, device_id=(grp, dev - 2), device_id_type=MESH)

    @pl.when(z < nz - 1)
    def _():
        pl.semaphore_signal(barrier, inc=1, device_id=(grp, dev + 2), device_id_type=MESH)

    mask = mask_ref[...].astype(jnp.float32)
    pieces = [mask[:, :main], mask[:, :main]]
    if tail:
        pieces += [mask[:, main:], mask[:, main:]]
    mask2 = jnp.concatenate(pieces, axis=1)
    lane = lax.broadcasted_iota(jnp.int32, (1, width), 1)
    first = (lane < main) | ((lane >= 2 * main) & (lane < 2 * main + tail))
    row0 = (grp * n_dev + dev) * rows

    def norm_rows(v):
        v = v.astype(jnp.float32)
        c = v - jnp.mean(v, axis=-1, keepdims=True)
        var = jnp.mean(c * c, axis=-1, keepdims=True)
        return (c * lax.rsqrt(var + EPSILON)).astype(jnp.bfloat16)

    def project(n, p, wg_t, wv_t, dst):
        nt = (((1,), (1,)), ((), ()))
        gate = lax.dot_general(wg_t, n, nt, preferred_element_type=jnp.float32)
        value = lax.dot_general(wv_t, n, nt, preferred_element_type=jnp.float32)
        m0 = mask_s[row0 + p].astype(jnp.float32)
        m1 = mask_s[row0 + half + p].astype(jnp.float32)
        m = mask2 * jnp.where(first, m0, m1)
        res = (sigmoid(gate) * value * m).astype(jnp.bfloat16)
        for k in range(n_plane):
            dst[k, p] = res[k * ch:(k + 1) * ch]

    wrg_t, wr_t = wrg_ref[...].T, wr_ref[...].T

    @pl.loop(0, half)
    def _(p):
        a, b = norm_rows(x_ref[p]), norm_rows(x_ref[p + half])
        parts = [a[:main], b[:main]]
        if tail:
            parts += [a[main:], b[main:]]
        n = jnp.concatenate(parts, axis=0)
        nbuf[p] = n
        project(n, p, wrg_t, wr_t, r_src)

    pl.semaphore_wait(
        barrier,
        n_plane - 1 + jnp.where(z > 0, 1, 0) + jnp.where(z < nz - 1, 1, 0),
    )

    def plane_copy(src, dst, send, recv, to):
        return pltpu.make_async_remote_copy(
            src_ref=src, dst_ref=dst, send_sem=send, recv_sem=recv,
            device_id=plane_peer(to), device_id_type=MESH)

    def z_copy(src, zz, s, up):
        return pltpu.make_async_remote_copy(
            src_ref=src, dst_ref=r_buf.at[zz, s], send_sem=z_send.at[1 if up else 0, zz, s],
            recv_sem=r_recv.at[zz, s], device_id=(grp, dev + (2 if up else -2)), device_id_type=MESH)

    def ra_copy(o):
        t = other_of(o)
        return plane_copy(r_src.at[t], r_buf.at[z, q], ra_send.at[o], r_recv.at[z, q], t)

    def l_copy(o):
        t = other_of(o)
        return plane_copy(l_src.at[t], l_buf.at[q], l_send.at[o], l_recv.at[q], t)

    def p_copy(t):
        return plane_copy(p_src.at[t], p_buf.at[q], p_send.at[t], p_recv.at[q], t)

    def wait_plane(dst, recv, s):
        plane_copy(dst, dst, recv, recv, s).wait_recv()

    @pl.when(z < nz - 1)
    def _():
        z_copy(r_src.at[q], z, q, True).start()

    @pl.when(z > 0)
    def _():
        z_copy(r_src.at[q], z, q, False).start()

    @pl.loop(1, n_plane)
    def _(o):
        ra_copy(o).start()

    own_r = pltpu.make_async_copy(r_src.at[q], r_buf.at[z, q], loc_sem.at[0])
    own_r.start()

    wlg_t, wl_t = wlg_ref[...].T, wl_ref[...].T

    @pl.loop(0, half)
    def _(p):
        project(nbuf[p], p, wlg_t, wl_t, l_src)

    @pl.loop(1, n_plane)
    def _(o):
        l_copy(o).start()

    own_l = pltpu.make_async_copy(l_src.at[q], l_buf.at[q], loc_sem.at[1])
    own_l.start()

    @pl.loop(1, n_plane)
    def _(o):
        s = other_of(o)
        wait_plane(r_buf.at[z, s], r_recv.at[z, s], s)

        @pl.when(z < nz - 1)
        def _():
            z_copy(r_buf.at[z, s], z, s, True).start()

        @pl.when(z > 0)
        def _():
            z_copy(r_buf.at[z, s], z, s, False).start()

    wog = wog_ref[...]

    @pl.loop(0, half)
    def _(p):
        g = sigmoid(jnp.dot(nbuf[p], wog, preferred_element_type=jnp.float32)).astype(jnp.bfloat16)
        out_ref[p, :main] = g[:main]
        out_ref[p + half, :main] = g[main:2 * main]
        if tail:
            out_ref[p, main:] = g[2 * main:2 * main + tail]
            out_ref[p + half, main:] = g[2 * main + tail:]

    lane1 = lax.broadcasted_iota(jnp.int32, (1, 128), 1)

    def unpack(block, s, masked):
        for p in range(half):
            v = block[p].astype(jnp.float32)
            for b in range(2):
                where = pl.ds(s * rows + p + b * half, ch, stride=plane_rows)
                for t in range(tiles):
                    stage[t, where, :] = v[:, b * main + t * 128:b * main + (t + 1) * 128]
                if tail:
                    u = v[:, 2 * main:]
                    if b:
                        u = pltpu.roll(u, tail, 1)
                    if masked:
                        u = jnp.where(lane1 < tail, u, 0.0)
                    stage[tiles, where, :] = u

    n_tiles = tiles + (1 if tail else 0)

    def settle(dst):
        for c in range(ch):
            for t in range(n_tiles):
                dst(c, t, stage[t, c * plane_rows:(c + 1) * plane_rows, :].astype(jnp.bfloat16))

    own_l.wait()

    @pl.loop(1, n_plane)
    def _(o):
        s = other_of(o)
        wait_plane(l_buf.at[s], l_recv.at[s], s)

    @pl.loop(0, n_plane)
    def _(s):
        unpack(l_buf.at[s], s, True)

    def to_left(c, t, v):
        l_mat[c, :, t * 128:(t + 1) * 128] = v

    settle(to_left)

    def take_plane(zz):
        @pl.loop(0, n_plane)
        def _(s):
            unpack(r_buf.at[zz, s], s, False)

        def to_right(c, t, v):
            r_mat[c, zz, :, t * 128:(t + 1) * 128] = v

        settle(to_right)

    own_r.wait()
    take_plane(z)

    @pl.loop(1, nz)
    def _(h):
        lo, hi = z - h, z + h

        @pl.loop(0, n_plane)
        def _(o):
            s = other_of(o)

            @pl.when(lo >= 0)
            def _():
                z_copy(r_buf.at[lo, s], lo, s, True).wait_recv()

                @pl.when(z < nz - 1)
                def _():
                    z_copy(r_buf.at[lo, s], lo, s, True).start()

            @pl.when(hi <= nz - 1)
            def _():
                z_copy(r_buf.at[hi, s], hi, s, False).wait_recv()

                @pl.when(z > 0)
                def _():
                    z_copy(r_buf.at[hi, s], hi, s, False).start()

        @pl.when(lo >= 0)
        def _():
            take_plane(lo)

        @pl.when(hi <= nz - 1)
        def _():
            take_plane(hi)

    for c in range(ch):
        prod = lax.dot_general(
            l_mat[c], r_mat[c].reshape(nz * plane_rows, n_tiles * 128), (((1,), (1,)), ((), ())),
            preferred_element_type=jnp.float32)
        for t in range(tiles):
            stage[t, c * plane_rows:(c + 1) * plane_rows, :] = prod[:, t * 128:(t + 1) * 128]
        if tail:
            stage[tiles, c * plane_rows:(c + 1) * plane_rows, :tail] = prod[:, main:]

    @pl.loop(1, n_plane + 1)
    def _(o):
        to = other_of(o)
        for p in range(half):
            pair = []
            ends = []
            for b in range(2):
                where = pl.ds(to * rows + p + b * half, ch, stride=plane_rows)
                pair += [stage[t, where, :] for t in range(tiles)]
                if tail:
                    ends.append(stage[tiles, where, :])
            if tail:
                pair.append(jnp.where(lane1 < tail, ends[0], pltpu.roll(ends[1], tail, 1)))
            p_src[to, p] = jnp.concatenate(pair, axis=1).astype(jnp.bfloat16)

        @pl.when(o < n_plane)
        def _():
            p_copy(to).start()

    own_p = pltpu.make_async_copy(p_src.at[q], p_buf.at[q], loc_sem.at[2])
    own_p.start()
    own_p.wait()

    @pl.loop(1, n_plane)
    def _(o):
        s = other_of(o)
        wait_plane(p_buf.at[s], p_recv.at[s], s)

    wo = wo_ref[...]
    piece = 2 * rows

    @pl.loop(0, half)
    def _(p):
        v = jnp.concatenate([p_buf[k, p] for k in range(n_plane)], axis=0).astype(jnp.float32)
        c = v - jnp.mean(v, axis=0, keepdims=True)
        var = jnp.mean(c * c, axis=0, keepdims=True)
        n = (c * lax.rsqrt(var + EPSILON)).astype(jnp.bfloat16)
        y = lax.dot_general(n, wo, (((0,), (0,)), ((), ())), preferred_element_type=jnp.float32)
        for b in range(2):
            parts = [y[b * main:(b + 1) * main]]
            if tail:
                parts.append(y[2 * main + b * tail:2 * main + (b + 1) * tail])
            full = jnp.concatenate(parts, axis=0)
            for zz in range(nz):
                for gg in range(n_grp):
                    y_buf[b, (gg * nz + zz) * piece:(gg * nz + zz + 1) * piece, :] = (
                        full[(zz * n_grp + gg) * piece:(zz * n_grp + gg + 1) * piece])
            row = p + b * half
            out_ref[row] = (y_buf[b] * out_ref[row].astype(jnp.float32)).astype(jnp.bfloat16)

    @pl.loop(1, n_plane)
    def _(o):
        ra_copy(o).wait_send()
        l_copy(o).wait_send()
        p_copy(other_of(o)).wait_send()

    @pl.loop(0, nz)
    def _(zz):
        @pl.loop(0, n_plane)
        def _(s):
            @pl.when((zz <= z) & (z < nz - 1))
            def _():
                z_copy(r_buf.at[zz, s], zz, s, True).wait_send()

            @pl.when((zz >= z) & (z > 0))
            def _():
                z_copy(r_buf.at[zz, s], zz, s, False).wait_send()


def fused(mesh, args):
    n_grp, n_dev = mesh.shape["grp"], mesh.shape["dev"]
    x, residue_mask = args[0], args[-1]
    rows, tokens, chans = x.shape
    n_plane, nz, half = n_grp * 2, n_dev // 2, rows // 2
    ch = args[1].shape[1] // n_plane
    width = 2 * tokens
    n_tiles = -(-tokens // 128)
    bf, f32 = jnp.bfloat16, jnp.float32
    blocks = (n_plane, half, ch, width)
    vmem = pl.BlockSpec(memory_space=pltpu.VMEM)
    dma = pltpu.SemaphoreType.DMA
    return pl.pallas_call(
        functools.partial(fused_kernel, n_grp, n_dev),
        out_shape=jax.ShapeDtypeStruct(x.shape, bf),
        in_specs=[vmem] * 8 + [pl.BlockSpec(memory_space=pltpu.SMEM)],
        out_specs=vmem,
        scratch_shapes=[
            pltpu.VMEM((half, width, chans), bf),
            pltpu.VMEM(blocks, bf),
            pltpu.VMEM(blocks, bf),
            pltpu.VMEM(blocks, bf),
            pltpu.VMEM((nz,) + blocks, bf),
            pltpu.VMEM(blocks, bf),
            pltpu.VMEM(blocks, bf),
            pltpu.VMEM((n_tiles, ch * n_plane * rows, 128), f32),
            pltpu.VMEM((ch, n_plane * rows, n_tiles * 128), bf),
            pltpu.VMEM((ch, nz, n_plane * rows, n_tiles * 128), bf),
            pltpu.VMEM((2, tokens, chans), f32),
            dma((n_plane,)),
            dma((n_plane,)),
            dma((n_plane,)),
            dma((2, nz, n_plane)),
            dma((nz, n_plane)),
            dma((n_plane,)),
            dma((n_plane,)),
            dma((3,)),
        ],
        compiler_params=pltpu.CompilerParams(
            collective_id=0, has_side_effects=True, vmem_limit_bytes=48 * 1024 * 1024),
        cost_estimate=pl.CostEstimate(flops=10**9, bytes_accessed=10**7, transcendentals=10**6),
    )(*args[:-1], residue_mask.reshape(1, tokens), residue_mask)


def fits(mesh, tokens, hidden):
    n_plane, nz = mesh.shape["grp"] * 2, mesh.shape["dev"] // 2
    rows = tokens // (n_plane * nz)
    if mesh.shape["dev"] % 2 or hidden % n_plane or (hidden // n_plane) % 16:
        return False
    if rows % 2 or (n_plane * rows) % 16 or tokens % 128 not in (0, 64):
        return False
    return 4 * (hidden // n_plane) * tokens * tokens < 16 * 1024 * 1024


def solution(mesh):
    def body(*args):
        if fits(mesh, args[-1].shape[0], args[1].shape[1]):
            return fused(mesh, args)
        return local(*args)

    return jax.shard_map(
        body,
        mesh=mesh,
        in_specs=(P(("grp", "dev"), None, None), P(), P(), P(), P(), P(), P(), P()),
        out_specs=P(("grp", "dev"), None, None),
        check_vma=False,
    )
```

```python
import functools

import jax
import jax.numpy as jnp
from jax import lax
from jax.experimental import pallas as pl
from jax.experimental.pallas import tpu as pltpu
from jax.sharding import PartitionSpec as P

EPSILON = 1e-05


def layer_norm(values, channel_axis):
    average = jnp.mean(values, axis=channel_axis, keepdims=True)
    centered = values - average
    variance = jnp.mean(centered * centered, axis=channel_axis, keepdims=True)
    return centered * lax.rsqrt(variance + EPSILON)


def gated_proj(normed, weight_gate, weight_value, pair_mask):
    gate_logits = jnp.einsum("rkc,cf->frk", normed, weight_gate, preferred_element_type=jnp.float32)
    projected = jnp.einsum("rkc,cf->frk", normed, weight_value, preferred_element_type=jnp.float32)
    return (jax.nn.sigmoid(gate_logits) * projected * pair_mask[None]).astype(jnp.bfloat16)


def local(pair_repr, w_left_gate, w_left, w_right_gate, w_right, w_out_gate, w_out, residue_mask):
    height = pair_repr.shape[0]
    row_start = (lax.axis_index("grp") * lax.axis_size("dev") + lax.axis_index("dev")) * height
    mask_float = residue_mask.astype(jnp.float32)
    row_mask = lax.dynamic_slice_in_dim(mask_float, row_start, height)
    pair_mask = row_mask[:, None] * mask_float[None, :]
    normed = layer_norm(pair_repr.astype(jnp.float32), 2).astype(jnp.bfloat16)
    left_rows = gated_proj(normed, w_left_gate, w_left, pair_mask)
    right_rows = gated_proj(normed, w_right_gate, w_right, pair_mask)
    out_gate = jax.nn.sigmoid(
        jnp.einsum("rkc,cd->rkd", normed, w_out_gate, preferred_element_type=jnp.float32)
    ).astype(jnp.bfloat16)
    left_cols, right_cols = (
        lax.all_to_all(left_rows, ("grp", "dev"), split_axis=0, concat_axis=1, tiled=True),
        lax.all_to_all(right_rows, ("grp", "dev"), split_axis=0, concat_axis=1, tiled=True),
    )
    product = jnp.einsum(
        "crk,csk->crs", left_cols, right_cols, preferred_element_type=jnp.float32
    ).astype(jnp.bfloat16)
    finish_product = lax.all_to_all(
        product, ("grp", "dev"), split_axis=1, concat_axis=0, tiled=True
    )
    normed_product = layer_norm(finish_product.astype(jnp.float32), 0).astype(jnp.bfloat16)
    mixed_rows = jnp.einsum(
        "crk,cd->rkd", normed_product, w_out, preferred_element_type=jnp.float32
    )
    return (mixed_rows * out_gate).astype(jnp.bfloat16)


MESH = pl.DeviceIdType.MESH
HALVES = 2
PLANES = 4


def sigmoid(x):
    return 1.0 / (1.0 + jnp.exp(-x))


def fused_kernel(
    n_grp, n_dev,
    x_hbm, wlg_hbm, wl_hbm, wrg_hbm, wr_hbm, wog_hbm, wo_hbm, mask_hbm,
    out_ref,
    x_ref, wlg_ref, wl_ref, wrg_ref, wr_ref, wog_ref, wo_ref, mask_ref, mask_s,
    nbuf, r_src, l_src, p_src, r_buf, l_buf, p_buf, stage, l_mat, r_mat, y_buf,
    ra_send, l_send, p_send, z_send, lz_send, r_recv, l_recv, p_recv, loc_sem, in_sem,
):
    rows, tokens, chans = x_ref.shape
    half = rows // 2
    _, n_plane, _, ch, width = r_src.shape
    nz = PLANES
    main = tokens // 128 * 128
    tail = tokens - main
    tiles = main // 128
    plane_rows = n_plane * rows
    grp = lax.axis_index("grp")
    dev = lax.axis_index("dev")
    z = dev // 2
    core = lax.rem(dev, 2)
    q = grp * 2 + core
    low = z < nz // 2
    inner = (z == 1) | (z == 2)
    outer = (z == 0) | (z == nz - 1)
    ahead = (grp, jnp.where(low, dev + 2, dev - 2))
    side = jnp.where(low, 0, nz - 1)
    own_inner = jnp.where(low, 1, 2)
    far_inner = nz - 1 - own_inner
    far_side = nz - 1 - side

    def plane_peer(other):
        return (other // 2, z * 2 + lax.rem(other, 2))

    def at_plane(other, zz):
        return (other // 2, zz * 2 + lax.rem(other, 2))

    def other_of(o):
        return lax.rem(q + o, n_plane)

    loads = [
        pltpu.make_async_copy(src, dst, in_sem.at[k])
        for k, (src, dst) in enumerate([
            (x_hbm, x_ref), (mask_hbm, mask_ref), (mask_hbm, mask_s), (wrg_hbm, wrg_ref), (wr_hbm, wr_ref),
            (wlg_hbm, wlg_ref), (wl_hbm, wl_ref), (wog_hbm, wog_ref), (wo_hbm, wo_ref)])
    ]
    for load in loads:
        load.start()

    barrier = pltpu.get_barrier_semaphore()

    @pl.loop(1, n_plane)
    def _(o):
        pl.semaphore_signal(barrier, inc=1, device_id=plane_peer(other_of(o)), device_id_type=MESH)

    @pl.when(inner)
    def _():
        pl.semaphore_signal(barrier, inc=1, device_id=ahead, device_id_type=MESH)
        pl.semaphore_signal(barrier, inc=1, device_id=at_plane(q, side), device_id_type=MESH)

    @pl.when(outer)
    def _():
        @pl.loop(0, n_plane)
        def _(k):
            pl.semaphore_signal(barrier, inc=1, device_id=at_plane(k, own_inner), device_id_type=MESH)

    for load in loads[:5]:
        load.wait()
    mask = mask_ref[...].astype(jnp.float32).reshape(1, tokens)
    pieces = [mask[:, :main], mask[:, :main]]
    if tail:
        pieces += [mask[:, main:], mask[:, main:]]
    mask2 = jnp.concatenate(pieces, axis=1)
    lane = lax.broadcasted_iota(jnp.int32, (1, width), 1)
    first = (lane < main) | ((lane >= 2 * main) & (lane < 2 * main + tail))
    row0 = (grp * n_dev + dev) * rows

    def norm_rows(v):
        v = v.astype(jnp.float32)
        c = v - jnp.mean(v, axis=-1, keepdims=True)
        var = jnp.mean(c * c, axis=-1, keepdims=True)
        return (c * lax.rsqrt(var + EPSILON)).astype(jnp.bfloat16)

    def project(n, p, wg_t, wv_t, dst):
        nt = (((1,), (1,)), ((), ()))
        gate = lax.dot_general(wg_t, n, nt, preferred_element_type=jnp.float32)
        value = lax.dot_general(wv_t, n, nt, preferred_element_type=jnp.float32)
        m0 = mask_s[row0 + p].astype(jnp.float32)
        m1 = mask_s[row0 + half + p].astype(jnp.float32)
        m = mask2 * jnp.where(first, m0, m1)
        res = (sigmoid(gate) * value * m).astype(jnp.bfloat16)
        for k in range(n_plane):
            for f in range(HALVES):
                lo = (k * HALVES + f) * ch
                dst[f, k, p] = res[lo:lo + ch]

    wrg_t, wr_t = wrg_ref[...].T, wr_ref[...].T

    @pl.loop(0, half)
    def _(p):
        a, b = norm_rows(x_ref[p]), norm_rows(x_ref[p + half])
        parts = [a[:main], b[:main]]
        if tail:
            parts += [a[main:], b[main:]]
        n = jnp.concatenate(parts, axis=0)
        nbuf[p] = n
        project(n, p, wrg_t, wr_t, r_src)

    pl.semaphore_wait(barrier, n_plane - 1 + jnp.where(inner, 1 + n_plane, 1))

    def plane_copy(src, dst, send, recv, to):
        return pltpu.make_async_remote_copy(
            src_ref=src, dst_ref=dst, send_sem=send, recv_sem=recv,
            device_id=plane_peer(to), device_id_type=MESH)

    def z_copy(src, f, zz, s):
        return pltpu.make_async_remote_copy(
            src_ref=src, dst_ref=r_buf.at[f, zz, s], send_sem=z_send.at[f, zz, s],
            recv_sem=r_recv.at[f, zz, s], device_id=ahead, device_id_type=MESH)

    def lz_copy(f, s):
        return pltpu.make_async_remote_copy(
            src_ref=l_buf.at[f, 0, s], dst_ref=l_buf.at[f, 1, s], send_sem=lz_send.at[f, s],
            recv_sem=l_recv.at[f, 1, s], device_id=ahead, device_id_type=MESH)

    def ra_copy(f, o):
        t = other_of(o)
        return plane_copy(r_src.at[f, t], r_buf.at[f, z, q], ra_send.at[f, o], r_recv.at[f, z, q], t)

    def l_copy(f, o):
        t = other_of(o)
        return plane_copy(l_src.at[f, t], l_buf.at[f, 0, q], l_send.at[f, o], l_recv.at[f, 0, q], t)

    def p_copy(f, w, t):
        return pltpu.make_async_remote_copy(
            src_ref=p_src.at[f, w, t], dst_ref=p_buf.at[f, q], send_sem=p_send.at[f, w, t],
            recv_sem=p_recv.at[f, q], device_id=at_plane(t, side if w else z), device_id_type=MESH)

    def wait_on(dst, recv):
        pltpu.make_async_remote_copy(
            src_ref=dst, dst_ref=dst, send_sem=recv, recv_sem=recv,
            device_id=ahead, device_id_type=MESH).wait_recv()

    def send_plane(f):
        @pl.loop(1, n_plane)
        def _(o):
            ra_copy(f, o).start()

    def send_left(f):
        @pl.loop(1, n_plane)
        def _(o):
            l_copy(f, o).start()

    send_plane(0)
    z_copy(r_src.at[0, q], 0, z, q).start()
    own_r = [pltpu.make_async_copy(r_src.at[f, q], r_buf.at[f, z, q], loc_sem.at[f]) for f in range(HALVES)]
    for copy in own_r:
        copy.start()

    for load in loads[5:]:
        load.wait()
    wlg_t, wl_t = wlg_ref[...].T, wl_ref[...].T

    @pl.loop(0, half)
    def _(p):
        project(nbuf[p], p, wlg_t, wl_t, l_src)

    own_l = [pltpu.make_async_copy(l_src.at[f, q], l_buf.at[f, 0, q], loc_sem.at[HALVES + f]) for f in range(HALVES)]
    for copy in own_l:
        copy.start()

    @pl.loop(1, n_plane)
    def _(o):
        s = other_of(o)
        wait_on(r_buf.at[0, z, s], r_recv.at[0, z, s])
        z_copy(r_buf.at[0, z, s], 0, z, s).start()

    send_left(0)

    wog = wog_ref[...]

    @pl.loop(0, half)
    def _(p):
        g = sigmoid(jnp.dot(nbuf[p], wog, preferred_element_type=jnp.float32)).astype(jnp.bfloat16)
        out_ref[p, :main] = g[:main]
        out_ref[p + half, :main] = g[main:2 * main]
        if tail:
            out_ref[p, main:] = g[2 * main:2 * main + tail]
            out_ref[p + half, main:] = g[2 * main + tail:]

    lane1 = lax.broadcasted_iota(jnp.int32, (1, 128), 1)

    def unpack(block, s, masked):
        for p in range(half):
            v = block[p].astype(jnp.float32)
            for b in range(2):
                where = pl.ds(s * rows + p + b * half, ch, stride=plane_rows)
                for t in range(tiles):
                    stage[t, where, :] = v[:, b * main + t * 128:b * main + (t + 1) * 128]
                if tail:
                    u = v[:, 2 * main:]
                    if b:
                        u = pltpu.roll(u, tail, 1)
                    if masked:
                        u = jnp.where(lane1 < tail, u, 0.0)
                    stage[tiles, where, :] = u

    n_tiles = tiles + (1 if tail else 0)

    def settle(dst):
        for c in range(ch):
            for t in range(n_tiles):
                dst(c, t, stage[t, c * plane_rows:(c + 1) * plane_rows, :].astype(jnp.bfloat16))

    for copy in own_r + own_l:
        copy.wait()

    def wait_left(f):
        @pl.loop(1, n_plane)
        def _(o):
            s = other_of(o)
            wait_on(l_buf.at[f, 0, s], l_recv.at[f, 0, s])

    def wait_right(f):
        @pl.loop(1, n_plane)
        def _(o):
            s = other_of(o)
            wait_on(r_buf.at[f, z, s], r_recv.at[f, z, s])

    wait_left(0)
    for f in range(1, HALVES):
        send_plane(f)

    @pl.when(outer)
    def _():
        @pl.loop(0, n_plane)
        def _(s):
            lz_copy(0, s).start()

    for f in range(1, HALVES):
        wait_right(f)
        send_left(f)

    @pl.when(outer)
    def _():
        for f in range(1, HALVES):
            @pl.loop(0, n_plane)
            def _(s):
                z_copy(r_buf.at[f - 1, z, s], f - 1, z, s).wait_send()

            @pl.loop(0, n_plane)
            def _(s):
                z_copy(r_buf.at[f, z, s], f, z, s).start()

            wait_left(f)

            @pl.loop(0, n_plane)
            def _(s):
                lz_copy(f - 1, s).wait_send()

            @pl.loop(0, n_plane)
            def _(s):
                lz_copy(f, s).start()

        @pl.loop(0, n_plane)
        def _(s):
            z_copy(r_buf.at[HALVES - 1, z, s], HALVES - 1, z, s).wait_send()
            lz_copy(HALVES - 1, s).wait_send()

    def take_left(f, w):
        @pl.loop(0, n_plane)
        def _(s):
            unpack(l_buf.at[f, w, s], s, True)

        def to_left(c, t, v):
            l_mat[c, :, t * 128:(t + 1) * 128] = v

        settle(to_left)

    def take_plane(f, zz):
        @pl.loop(0, n_plane)
        def _(s):
            unpack(r_buf.at[f, zz, s], s, False)

        def to_right(c, t, v):
            r_mat[c, zz, :, t * 128:(t + 1) * 128] = v

        settle(to_right)

    def multiply(f, w):
        for c in range(ch):
            prod = lax.dot_general(
                l_mat[c], r_mat[c].reshape(nz * plane_rows, n_tiles * 128), (((1,), (1,)), ((), ())),
                preferred_element_type=jnp.float32)
            for t in range(tiles):
                stage[t, c * plane_rows:(c + 1) * plane_rows, :] = prod[:, t * 128:(t + 1) * 128]
            if tail:
                stage[tiles, c * plane_rows:(c + 1) * plane_rows, :tail] = prod[:, main:]

        @pl.loop(1, n_plane + 1)
        def _(o):
            to = other_of(o)
            for p in range(half):
                pair = []
                ends = []
                for b in range(2):
                    where = pl.ds(to * rows + p + b * half, ch, stride=plane_rows)
                    pair += [stage[t, where, :] for t in range(tiles)]
                    if tail:
                        ends.append(stage[tiles, where, :])
                if tail:
                    pair.append(jnp.where(lane1 < tail, ends[0], pltpu.roll(ends[1], tail, 1)))
                p_src[f, w, to, p] = jnp.concatenate(pair, axis=1).astype(jnp.bfloat16)

            if w:
                p_copy(f, w, to).start()
            else:
                @pl.when(o < n_plane)
                def _():
                    p_copy(f, w, to).start()

    def local_p(f):
        return pltpu.make_async_copy(p_src.at[f, 0, q], p_buf.at[f, q], loc_sem.at[2 * HALVES + f])

    @pl.when(inner)
    def _():
        for f in range(HALVES):
            take_plane(f, z)

            @pl.loop(0, n_plane)
            def _(s):
                wait_on(r_buf.at[f, side, s], r_recv.at[f, side, s])
                z_copy(r_buf.at[f, side, s], f, side, s).start()

            take_plane(f, side)

            @pl.loop(0, n_plane)
            def _(s):
                wait_on(r_buf.at[f, far_inner, s], r_recv.at[f, far_inner, s])

            take_plane(f, far_inner)

            @pl.loop(0, n_plane)
            def _(s):
                wait_on(r_buf.at[f, far_side, s], r_recv.at[f, far_side, s])

            if f + 1 < HALVES:
                @pl.loop(0, n_plane)
                def _(s):
                    z_copy(r_buf.at[f + 1, z, s], f + 1, z, s).start()

                wait_left(f + 1)

            take_plane(f, far_side)

            @pl.loop(0, n_plane)
            def _(s):
                wait_on(l_buf.at[f, 1, s], l_recv.at[f, 1, s])

            take_left(f, 1)
            multiply(f, 1)
            take_left(f, 0)
            multiply(f, 0)
            local_p(f).start()

        for f in range(HALVES):
            local_p(f).wait()

            @pl.loop(1, n_plane)
            def _(o):
                s = other_of(o)
                wait_on(p_buf.at[f, s], p_recv.at[f, s])

    @pl.when(outer)
    def _():
        for f in range(HALVES):
            @pl.loop(0, n_plane)
            def _(s):
                wait_on(p_buf.at[f, s], p_recv.at[f, s])

    wo = wo_ref[...]
    piece = 2 * rows

    @pl.loop(0, half)
    def _(p):
        v = jnp.concatenate(
            [p_buf[f, k, p].astype(jnp.float32) for k in range(n_plane) for f in range(HALVES)], axis=0)
        c = v - jnp.mean(v, axis=0, keepdims=True)
        var = jnp.mean(c * c, axis=0, keepdims=True)
        n = (c * lax.rsqrt(var + EPSILON)).astype(jnp.bfloat16)
        y = lax.dot_general(n, wo, (((0,), (0,)), ((), ())), preferred_element_type=jnp.float32)
        for b in range(2):
            parts = [y[b * main:(b + 1) * main]]
            if tail:
                parts.append(y[2 * main + b * tail:2 * main + (b + 1) * tail])
            full = jnp.concatenate(parts, axis=0)
            for zz in range(nz):
                for gg in range(n_grp):
                    y_buf[b, (gg * nz + zz) * piece:(gg * nz + zz + 1) * piece, :] = (
                        full[(zz * n_grp + gg) * piece:(zz * n_grp + gg + 1) * piece])
            row = p + b * half
            out_ref[row] = (y_buf[b] * out_ref[row].astype(jnp.float32)).astype(jnp.bfloat16)

    for f in range(HALVES):
        @pl.loop(1, n_plane)
        def _(o):
            ra_copy(f, o).wait_send()
            l_copy(f, o).wait_send()

        @pl.when(inner)
        def _():
            @pl.loop(1, n_plane)
            def _(o):
                p_copy(f, 0, other_of(o)).wait_send()

            @pl.loop(0, n_plane)
            def _(s):
                p_copy(f, 1, s).wait_send()
                z_copy(r_buf.at[f, z, s], f, z, s).wait_send()
                z_copy(r_buf.at[f, side, s], f, side, s).wait_send()


def fused(mesh, args):
    n_grp, n_dev = mesh.shape["grp"], mesh.shape["dev"]
    x = args[0]
    rows, tokens, chans = x.shape
    n_plane, nz, half = n_grp * 2, n_dev // 2, rows // 2
    ch = args[1].shape[1] // n_plane // HALVES
    width = 2 * tokens
    n_tiles = -(-tokens // 128)
    bf, f32 = jnp.bfloat16, jnp.float32
    blocks = (n_plane, half, ch, width)
    whole = (HALVES,) + blocks
    weight = pltpu.VMEM(args[1].shape, bf)
    hbm = pl.BlockSpec(memory_space=pltpu.HBM)
    vmem = pl.BlockSpec(memory_space=pltpu.VMEM)
    dma = pltpu.SemaphoreType.DMA
    return pl.pallas_call(
        functools.partial(fused_kernel, n_grp, n_dev),
        out_shape=jax.ShapeDtypeStruct(x.shape, bf),
        in_specs=[hbm] * 8,
        out_specs=vmem,
        scratch_shapes=[
            pltpu.VMEM(x.shape, bf),
            weight, weight, weight, weight, weight, weight,
            pltpu.VMEM((tokens,), jnp.int32),
            pltpu.SMEM((tokens,), jnp.int32),
            pltpu.VMEM((half, width, chans), bf),
            pltpu.VMEM(whole, bf),
            pltpu.VMEM(whole, bf),
            pltpu.VMEM((HALVES, 2) + blocks, bf),
            pltpu.VMEM((HALVES, nz) + blocks, bf),
            pltpu.VMEM((HALVES, 2) + blocks, bf),
            pltpu.VMEM(whole, bf),
            pltpu.VMEM((n_tiles, ch * n_plane * rows, 128), f32),
            pltpu.VMEM((ch, n_plane * rows, n_tiles * 128), bf),
            pltpu.VMEM((ch, nz, n_plane * rows, n_tiles * 128), bf),
            pltpu.VMEM((2, tokens, chans), f32),
            dma((HALVES, n_plane)),
            dma((HALVES, n_plane)),
            dma((HALVES, 2, n_plane)),
            dma((HALVES, nz, n_plane)),
            dma((HALVES, n_plane)),
            dma((HALVES, nz, n_plane)),
            dma((HALVES, 2, n_plane)),
            dma((HALVES, n_plane)),
            dma((3 * HALVES,)),
            dma((9,)),
        ],
        compiler_params=pltpu.CompilerParams(
            collective_id=0, has_side_effects=True, vmem_limit_bytes=56 * 1024 * 1024),
        cost_estimate=pl.CostEstimate(flops=10**9, bytes_accessed=10**7, transcendentals=10**6),
    )(*args)


def fits(mesh, tokens, hidden):
    n_plane, nz = mesh.shape["grp"] * 2, mesh.shape["dev"] // 2
    rows = tokens // (n_plane * nz)
    if mesh.shape["dev"] != 2 * PLANES or hidden % n_plane or (hidden // n_plane) % 16:
        return False
    if rows % 2 or (n_plane * rows) % 16 or tokens % 128 not in (0, 64):
        return False
    return 4 * (hidden // n_plane) * tokens * tokens < 16 * 1024 * 1024


def solution(mesh):
    def body(*args):
        if fits(mesh, args[-1].shape[0], args[1].shape[1]):
            return fused(mesh, args)
        return local(*args)

    return jax.shard_map(
        body,
        mesh=mesh,
        in_specs=(P(("grp", "dev"), None, None), P(), P(), P(), P(), P(), P(), P()),
        out_specs=P(("grp", "dev"), None, None),
        check_vma=False,
    )
```

```python
import functools

import jax
import jax.numpy as jnp
from jax import lax
from jax.experimental import pallas as pl
from jax.experimental.pallas import tpu as pltpu
from jax.sharding import PartitionSpec as P

EPSILON = 1e-05


def layer_norm(values, channel_axis):
    average = jnp.mean(values, axis=channel_axis, keepdims=True)
    centered = values - average
    variance = jnp.mean(centered * centered, axis=channel_axis, keepdims=True)
    return centered * lax.rsqrt(variance + EPSILON)


def gated_proj(normed, weight_gate, weight_value, pair_mask):
    gate_logits = jnp.einsum("rkc,cf->frk", normed, weight_gate, preferred_element_type=jnp.float32)
    projected = jnp.einsum("rkc,cf->frk", normed, weight_value, preferred_element_type=jnp.float32)
    return (jax.nn.sigmoid(gate_logits) * projected * pair_mask[None]).astype(jnp.bfloat16)


def local(pair_repr, w_left_gate, w_left, w_right_gate, w_right, w_out_gate, w_out, residue_mask):
    height = pair_repr.shape[0]
    row_start = (lax.axis_index("grp") * lax.axis_size("dev") + lax.axis_index("dev")) * height
    mask_float = residue_mask.astype(jnp.float32)
    row_mask = lax.dynamic_slice_in_dim(mask_float, row_start, height)
    pair_mask = row_mask[:, None] * mask_float[None, :]
    normed = layer_norm(pair_repr.astype(jnp.float32), 2).astype(jnp.bfloat16)
    left_rows = gated_proj(normed, w_left_gate, w_left, pair_mask)
    right_rows = gated_proj(normed, w_right_gate, w_right, pair_mask)
    out_gate = jax.nn.sigmoid(
        jnp.einsum("rkc,cd->rkd", normed, w_out_gate, preferred_element_type=jnp.float32)
    ).astype(jnp.bfloat16)
    left_cols, right_cols = (
        lax.all_to_all(left_rows, ("grp", "dev"), split_axis=0, concat_axis=1, tiled=True),
        lax.all_to_all(right_rows, ("grp", "dev"), split_axis=0, concat_axis=1, tiled=True),
    )
    product = jnp.einsum(
        "crk,csk->crs", left_cols, right_cols, preferred_element_type=jnp.float32
    ).astype(jnp.bfloat16)
    finish_product = lax.all_to_all(
        product, ("grp", "dev"), split_axis=1, concat_axis=0, tiled=True
    )
    normed_product = layer_norm(finish_product.astype(jnp.float32), 0).astype(jnp.bfloat16)
    mixed_rows = jnp.einsum(
        "crk,cd->rkd", normed_product, w_out, preferred_element_type=jnp.float32
    )
    return (mixed_rows * out_gate).astype(jnp.bfloat16)


MESH = pl.DeviceIdType.MESH
HALVES = 2
PLANES = 4


def sigmoid(x):
    return 1.0 / (1.0 + jnp.exp(-x))


def fused_kernel(
    n_grp, n_dev,
    x_hbm, wlg_hbm, wl_hbm, wrg_hbm, wr_hbm, wog_hbm, wo_hbm, mask_hbm,
    out_ref,
    x_ref, wlg_ref, wl_ref, wrg_ref, wr_ref, wog_ref, wo_ref, mask_ref, mask_s,
    nbuf, r_src, l_src, p_src, r_buf, l_buf, p_buf, stage, l_mat, r_mat, y_buf,
    ra_send, l_send, p_send, z_send, lz_send, r_recv, l_recv, p_recv, loc_sem, in_sem,
):
    rows, tokens, chans = x_ref.shape
    half = rows // 2
    _, n_plane, _, ch, width = r_src.shape
    nz = PLANES
    main = tokens // 128 * 128
    tail = tokens - main
    tiles = main // 128
    plane_rows = n_plane * rows
    grp = lax.axis_index("grp")
    dev = lax.axis_index("dev")
    z = dev // 2
    core = lax.rem(dev, 2)
    q = grp * 2 + core
    low = z < nz // 2
    inner = (z == 1) | (z == 2)
    outer = (z == 0) | (z == nz - 1)
    ahead = (grp, jnp.where(low, dev + 2, dev - 2))
    side = jnp.where(low, 0, nz - 1)
    own_inner = jnp.where(low, 1, 2)
    far_inner = nz - 1 - own_inner
    far_side = nz - 1 - side

    def plane_peer(other):
        return (other // 2, z * 2 + lax.rem(other, 2))

    def at_plane(other, zz):
        return (other // 2, zz * 2 + lax.rem(other, 2))

    def other_of(o):
        return lax.rem(q + o, n_plane)

    loads = [
        pltpu.make_async_copy(src, dst, in_sem.at[k])
        for k, (src, dst) in enumerate([
            (x_hbm, x_ref), (mask_hbm, mask_ref), (mask_hbm, mask_s), (wrg_hbm, wrg_ref), (wr_hbm, wr_ref),
            (wlg_hbm, wlg_ref), (wl_hbm, wl_ref), (wog_hbm, wog_ref), (wo_hbm, wo_ref)])
    ]
    for load in loads:
        load.start()

    barrier = pltpu.get_barrier_semaphore()

    @pl.loop(1, n_plane)
    def _(o):
        pl.semaphore_signal(barrier, inc=1, device_id=plane_peer(other_of(o)), device_id_type=MESH)

    @pl.when(inner)
    def _():
        pl.semaphore_signal(barrier, inc=1, device_id=ahead, device_id_type=MESH)
        pl.semaphore_signal(barrier, inc=1, device_id=at_plane(q, side), device_id_type=MESH)

    @pl.when(outer)
    def _():
        @pl.loop(0, n_plane)
        def _(k):
            pl.semaphore_signal(barrier, inc=1, device_id=at_plane(k, own_inner), device_id_type=MESH)

    for load in loads[:5]:
        load.wait()
    mask = mask_ref[...].astype(jnp.float32).reshape(1, tokens)
    pieces = [mask[:, :main], mask[:, :main]]
    if tail:
        pieces += [mask[:, main:], mask[:, main:]]
    mask2 = jnp.concatenate(pieces, axis=1)
    lane = lax.broadcasted_iota(jnp.int32, (1, width), 1)
    first = (lane < main) | ((lane >= 2 * main) & (lane < 2 * main + tail))
    row0 = (grp * n_dev + dev) * rows

    def norm_rows(v):
        v = v.astype(jnp.float32)
        c = v - jnp.mean(v, axis=-1, keepdims=True)
        var = jnp.mean(c * c, axis=-1, keepdims=True)
        return (c * lax.rsqrt(var + EPSILON)).astype(jnp.bfloat16)

    def project(n, p, wg_t, wv_t, dst):
        nt = (((1,), (1,)), ((), ()))
        gate = lax.dot_general(wg_t, n, nt, preferred_element_type=jnp.float32)
        value = lax.dot_general(wv_t, n, nt, preferred_element_type=jnp.float32)
        m0 = mask_s[row0 + p].astype(jnp.float32)
        m1 = mask_s[row0 + half + p].astype(jnp.float32)
        m = mask2 * jnp.where(first, m0, m1)
        res = (sigmoid(gate) * value * m).astype(jnp.bfloat16)
        for k in range(n_plane):
            for f in range(HALVES):
                lo = (k * HALVES + f) * ch
                dst[f, k, p] = res[lo:lo + ch]

    wrg_t, wr_t = wrg_ref[...].T, wr_ref[...].T

    @pl.loop(0, half)
    def _(p):
        a, b = norm_rows(x_ref[p]), norm_rows(x_ref[p + half])
        parts = [a[:main], b[:main]]
        if tail:
            parts += [a[main:], b[main:]]
        n = jnp.concatenate(parts, axis=0)
        nbuf[p] = n
        project(n, p, wrg_t, wr_t, r_src)

    pl.semaphore_wait(barrier, n_plane - 1 + jnp.where(inner, 1 + n_plane, 1))

    def plane_copy(src, dst, send, recv, to):
        return pltpu.make_async_remote_copy(
            src_ref=src, dst_ref=dst, send_sem=send, recv_sem=recv,
            device_id=plane_peer(to), device_id_type=MESH)

    def z_copy(src, f, zz, s):
        return pltpu.make_async_remote_copy(
            src_ref=src, dst_ref=r_buf.at[f, zz, s], send_sem=z_send.at[f, zz, s],
            recv_sem=r_recv.at[f, zz, s], device_id=ahead, device_id_type=MESH)

    def lz_copy(f, s):
        return pltpu.make_async_remote_copy(
            src_ref=l_buf.at[f, 0, s], dst_ref=l_buf.at[f, 1, s], send_sem=lz_send.at[f, s],
            recv_sem=l_recv.at[f, 1, s], device_id=ahead, device_id_type=MESH)

    def ra_copy(f, o):
        t = other_of(o)
        return plane_copy(r_src.at[f, t], r_buf.at[f, z, q], ra_send.at[f, o], r_recv.at[f, z, q], t)

    def l_copy(f, o):
        t = other_of(o)
        return plane_copy(l_src.at[f, t], l_buf.at[f, 0, q], l_send.at[f, o], l_recv.at[f, 0, q], t)

    def p_copy(f, w, t):
        return pltpu.make_async_remote_copy(
            src_ref=p_src.at[f, w, t], dst_ref=p_buf.at[f, q], send_sem=p_send.at[f, w, t],
            recv_sem=p_recv.at[f, q], device_id=at_plane(t, side if w else z), device_id_type=MESH)

    def wait_on(dst, recv):
        pltpu.make_async_remote_copy(
            src_ref=dst, dst_ref=dst, send_sem=recv, recv_sem=recv,
            device_id=ahead, device_id_type=MESH).wait_recv()

    def send_plane(f):
        @pl.loop(1, n_plane)
        def _(o):
            ra_copy(f, o).start()

    def send_left(f):
        @pl.loop(1, n_plane)
        def _(o):
            l_copy(f, o).start()

    send_plane(0)
    z_copy(r_src.at[0, q], 0, z, q).start()
    own_r = [pltpu.make_async_copy(r_src.at[f, q], r_buf.at[f, z, q], loc_sem.at[f]) for f in range(HALVES)]
    for copy in own_r:
        copy.start()

    for load in loads[5:]:
        load.wait()
    wlg_t, wl_t = wlg_ref[...].T, wl_ref[...].T

    @pl.loop(0, half)
    def _(p):
        project(nbuf[p], p, wlg_t, wl_t, l_src)

    own_l = [pltpu.make_async_copy(l_src.at[f, q], l_buf.at[f, 0, q], loc_sem.at[HALVES + f]) for f in range(HALVES)]
    for copy in own_l:
        copy.start()

    send_left(0)

    @pl.loop(1, n_plane)
    def _(o):
        s = other_of(o)
        wait_on(r_buf.at[0, z, s], r_recv.at[0, z, s])
        z_copy(r_buf.at[0, z, s], 0, z, s).start()

    for f in range(1, HALVES):
        send_plane(f)
        send_left(f)

    wog = wog_ref[...]

    @pl.loop(0, half)
    def _(p):
        g = sigmoid(jnp.dot(nbuf[p], wog, preferred_element_type=jnp.float32)).astype(jnp.bfloat16)
        out_ref[p, :main] = g[:main]
        out_ref[p + half, :main] = g[main:2 * main]
        if tail:
            out_ref[p, main:] = g[2 * main:2 * main + tail]
            out_ref[p + half, main:] = g[2 * main + tail:]

    lane1 = lax.broadcasted_iota(jnp.int32, (1, 128), 1)

    def unpack(block, s, masked):
        for p in range(half):
            v = block[p].astype(jnp.float32)
            for b in range(2):
                where = pl.ds(s * rows + p + b * half, ch, stride=plane_rows)
                for t in range(tiles):
                    stage[t, where, :] = v[:, b * main + t * 128:b * main + (t + 1) * 128]
                if tail:
                    u = v[:, 2 * main:]
                    if b:
                        u = pltpu.roll(u, tail, 1)
                    if masked:
                        u = jnp.where(lane1 < tail, u, 0.0)
                    stage[tiles, where, :] = u

    n_tiles = tiles + (1 if tail else 0)

    def settle(dst):
        for c in range(ch):
            for t in range(n_tiles):
                dst(c, t, stage[t, c * plane_rows:(c + 1) * plane_rows, :].astype(jnp.bfloat16))

    for copy in own_r + own_l:
        copy.wait()

    def wait_left(f):
        @pl.loop(1, n_plane)
        def _(o):
            s = other_of(o)
            wait_on(l_buf.at[f, 0, s], l_recv.at[f, 0, s])

    def wait_right(f):
        @pl.loop(1, n_plane)
        def _(o):
            s = other_of(o)
            wait_on(r_buf.at[f, z, s], r_recv.at[f, z, s])

    wait_left(0)
    @pl.when(outer)
    def _():
        @pl.loop(0, n_plane)
        def _(s):
            lz_copy(0, s).start()

    for f in range(1, HALVES):
        wait_right(f)

    @pl.when(outer)
    def _():
        for f in range(1, HALVES):
            @pl.loop(0, n_plane)
            def _(s):
                z_copy(r_buf.at[f, z, s], f, z, s).start()

            wait_left(f)

            @pl.loop(0, n_plane)
            def _(s):
                lz_copy(f, s).start()

        for f in range(HALVES):
            @pl.loop(0, n_plane)
            def _(s):
                z_copy(r_buf.at[f, z, s], f, z, s).wait_send()
                lz_copy(f, s).wait_send()

    def take_left(f, w):
        @pl.loop(0, n_plane)
        def _(s):
            unpack(l_buf.at[f, w, s], s, True)

        def to_left(c, t, v):
            l_mat[c, :, t * 128:(t + 1) * 128] = v

        settle(to_left)

    def take_plane(f, zz):
        @pl.loop(0, n_plane)
        def _(s):
            unpack(r_buf.at[f, zz, s], s, False)

        def to_right(c, t, v):
            r_mat[c, zz, :, t * 128:(t + 1) * 128] = v

        settle(to_right)

    def multiply(f, w):
        for c in range(ch):
            prod = lax.dot_general(
                l_mat[c], r_mat[c].reshape(nz * plane_rows, n_tiles * 128), (((1,), (1,)), ((), ())),
                preferred_element_type=jnp.float32)
            for t in range(tiles):
                stage[t, c * plane_rows:(c + 1) * plane_rows, :] = prod[:, t * 128:(t + 1) * 128]
            if tail:
                stage[tiles, c * plane_rows:(c + 1) * plane_rows, :tail] = prod[:, main:]

        @pl.loop(1, n_plane + 1)
        def _(o):
            to = other_of(o)
            for p in range(half):
                pair = []
                ends = []
                for b in range(2):
                    where = pl.ds(to * rows + p + b * half, ch, stride=plane_rows)
                    pair += [stage[t, where, :] for t in range(tiles)]
                    if tail:
                        ends.append(stage[tiles, where, :])
                if tail:
                    pair.append(jnp.where(lane1 < tail, ends[0], pltpu.roll(ends[1], tail, 1)))
                p_src[f, w, to, p] = jnp.concatenate(pair, axis=1).astype(jnp.bfloat16)

            if w:
                p_copy(f, w, to).start()
            else:
                @pl.when(o < n_plane)
                def _():
                    p_copy(f, w, to).start()

    def local_p(f):
        return pltpu.make_async_copy(p_src.at[f, 0, q], p_buf.at[f, q], loc_sem.at[2 * HALVES + f])

    @pl.when(inner)
    def _():
        for f in range(HALVES):
            take_plane(f, z)

            @pl.loop(0, n_plane)
            def _(s):
                wait_on(r_buf.at[f, side, s], r_recv.at[f, side, s])
                z_copy(r_buf.at[f, side, s], f, side, s).start()

            take_plane(f, side)

            @pl.loop(0, n_plane)
            def _(s):
                wait_on(r_buf.at[f, far_inner, s], r_recv.at[f, far_inner, s])

            take_plane(f, far_inner)

            @pl.loop(0, n_plane)
            def _(s):
                wait_on(r_buf.at[f, far_side, s], r_recv.at[f, far_side, s])

            if f + 1 < HALVES:
                @pl.loop(0, n_plane)
                def _(s):
                    z_copy(r_buf.at[f + 1, z, s], f + 1, z, s).start()

                wait_left(f + 1)

            take_plane(f, far_side)

            @pl.loop(0, n_plane)
            def _(s):
                wait_on(l_buf.at[f, 1, s], l_recv.at[f, 1, s])

            take_left(f, 1)
            multiply(f, 1)
            take_left(f, 0)
            multiply(f, 0)
            local_p(f).start()

        for f in range(HALVES):
            local_p(f).wait()

            @pl.loop(1, n_plane)
            def _(o):
                s = other_of(o)
                wait_on(p_buf.at[f, s], p_recv.at[f, s])

    @pl.when(outer)
    def _():
        for f in range(HALVES):
            @pl.loop(0, n_plane)
            def _(s):
                wait_on(p_buf.at[f, s], p_recv.at[f, s])

    wo = wo_ref[...]
    piece = 2 * rows

    @pl.loop(0, half)
    def _(p):
        v = jnp.concatenate(
            [p_buf[f, k, p].astype(jnp.float32) for k in range(n_plane) for f in range(HALVES)], axis=0)
        c = v - jnp.mean(v, axis=0, keepdims=True)
        var = jnp.mean(c * c, axis=0, keepdims=True)
        n = (c * lax.rsqrt(var + EPSILON)).astype(jnp.bfloat16)
        y = lax.dot_general(n, wo, (((0,), (0,)), ((), ())), preferred_element_type=jnp.float32)
        for b in range(2):
            parts = [y[b * main:(b + 1) * main]]
            if tail:
                parts.append(y[2 * main + b * tail:2 * main + (b + 1) * tail])
            full = jnp.concatenate(parts, axis=0)
            for zz in range(nz):
                for gg in range(n_grp):
                    y_buf[b, (gg * nz + zz) * piece:(gg * nz + zz + 1) * piece, :] = (
                        full[(zz * n_grp + gg) * piece:(zz * n_grp + gg + 1) * piece])
            row = p + b * half
            out_ref[row] = (y_buf[b] * out_ref[row].astype(jnp.float32)).astype(jnp.bfloat16)

    for f in range(HALVES):
        @pl.loop(1, n_plane)
        def _(o):
            ra_copy(f, o).wait_send()
            l_copy(f, o).wait_send()

        @pl.when(inner)
        def _():
            @pl.loop(1, n_plane)
            def _(o):
                p_copy(f, 0, other_of(o)).wait_send()

            @pl.loop(0, n_plane)
            def _(s):
                p_copy(f, 1, s).wait_send()
                z_copy(r_buf.at[f, z, s], f, z, s).wait_send()
                z_copy(r_buf.at[f, side, s], f, side, s).wait_send()


def fused(mesh, args):
    n_grp, n_dev = mesh.shape["grp"], mesh.shape["dev"]
    x = args[0]
    rows, tokens, chans = x.shape
    n_plane, nz, half = n_grp * 2, n_dev // 2, rows // 2
    ch = args[1].shape[1] // n_plane // HALVES
    width = 2 * tokens
    n_tiles = -(-tokens // 128)
    bf, f32 = jnp.bfloat16, jnp.float32
    blocks = (n_plane, half, ch, width)
    whole = (HALVES,) + blocks
    weight = pltpu.VMEM(args[1].shape, bf)
    hbm = pl.BlockSpec(memory_space=pltpu.HBM)
    vmem = pl.BlockSpec(memory_space=pltpu.VMEM)
    dma = pltpu.SemaphoreType.DMA
    return pl.pallas_call(
        functools.partial(fused_kernel, n_grp, n_dev),
        out_shape=jax.ShapeDtypeStruct(x.shape, bf),
        in_specs=[hbm] * 8,
        out_specs=vmem,
        scratch_shapes=[
            pltpu.VMEM(x.shape, bf),
            weight, weight, weight, weight, weight, weight,
            pltpu.VMEM((tokens,), jnp.int32),
            pltpu.SMEM((tokens,), jnp.int32),
            pltpu.VMEM((half, width, chans), bf),
            pltpu.VMEM(whole, bf),
            pltpu.VMEM(whole, bf),
            pltpu.VMEM((HALVES, 2) + blocks, bf),
            pltpu.VMEM((HALVES, nz) + blocks, bf),
            pltpu.VMEM((HALVES, 2) + blocks, bf),
            pltpu.VMEM(whole, bf),
            pltpu.VMEM((n_tiles, ch * n_plane * rows, 128), f32),
            pltpu.VMEM((ch, n_plane * rows, n_tiles * 128), bf),
            pltpu.VMEM((ch, nz, n_plane * rows, n_tiles * 128), bf),
            pltpu.VMEM((2, tokens, chans), f32),
            dma((HALVES, n_plane)),
            dma((HALVES, n_plane)),
            dma((HALVES, 2, n_plane)),
            dma((HALVES, nz, n_plane)),
            dma((HALVES, n_plane)),
            dma((HALVES, nz, n_plane)),
            dma((HALVES, 2, n_plane)),
            dma((HALVES, n_plane)),
            dma((3 * HALVES,)),
            dma((9,)),
        ],
        compiler_params=pltpu.CompilerParams(
            collective_id=0, has_side_effects=True, vmem_limit_bytes=56 * 1024 * 1024),
        cost_estimate=pl.CostEstimate(flops=10**9, bytes_accessed=10**7, transcendentals=10**6),
    )(*args)


def fits(mesh, tokens, hidden):
    n_plane, nz = mesh.shape["grp"] * 2, mesh.shape["dev"] // 2
    rows = tokens // (n_plane * nz)
    if mesh.shape["dev"] != 2 * PLANES or hidden % n_plane or (hidden // n_plane) % 16:
        return False
    if rows % 2 or (n_plane * rows) % 16 or tokens % 128 not in (0, 64):
        return False
    return 4 * (hidden // n_plane) * tokens * tokens < 16 * 1024 * 1024


def solution(mesh):
    def body(*args):
        if fits(mesh, args[-1].shape[0], args[1].shape[1]):
            return fused(mesh, args)
        return local(*args)

    return jax.shard_map(
        body,
        mesh=mesh,
        in_specs=(P(("grp", "dev"), None, None), P(), P(), P(), P(), P(), P(), P()),
        out_specs=P(("grp", "dev"), None, None),
        check_vma=False,
    )
```
